256 devices in a mesh: dp: 16 (over x, z_hi, core), ctx: 16 (over y, z_lo).
Axes of the slice: x: 4, y: 4, z: 8 (z_hi: 2, z_lo: 4; z = z_hi * 4 + z_lo), core: 2. Of those that a mesh axis runs over, the one named last changes fastest.
Arguments:
- saved_input: bfloat16 [16, 4096, 2048], P('dp', None, 'ctx'), may hold values from -6 to 6
- out_gate: bfloat16 [16, 4096, 2048], P('dp', None, 'ctx'), may hold values from -6 to 6
- grad_out: bfloat16 [16, 4096, 2048], P('dp', None, 'ctx'), may hold values from -6 to 6
- long_filter: float32 [4096, 2048], P('ctx'), may hold values from -0.125 to 0.125
Outputs:
- grad_input: bfloat16 [16, 4096, 2048], P('dp', None, 'ctx')
- grad_filter: float32 [4096, 2048], P('ctx', 'dp')
The draws below stay inside these ranges and needn't reach their ends.
All inputs are finite; a program needn't handle non-finite values.
Results may differ from the reference program's by a relative error of at most 0.0085.
Values may be sent and summed in bfloat16 or wider, within the bound.
A program may use at most 128 MiB of HBM per device.

```python
import math
import jax
import jax.numpy as jnp
from jax import lax

CHANNELS = 4096
SEQ = 2048
BATCH = 16


def shard_levels(key, dims, split, smallest, largest):
    def one(axis_at, shards_of):
        heights = jax.random.uniform(jax.random.fold_in(jax.random.fold_in(key, 6), axis_at), (shards_of,), jnp.float32, smallest / len(split), largest / len(split))
        return jnp.repeat(jnp.exp(heights), dims[axis_at] // shards_of).reshape((-1,) + (1,) * (len(dims) - axis_at - 1))

    factor_of = one(*split[0])
    for cut in split[1:]:
        factor_of = factor_of * one(*cut)
    return factor_of


def bell_draw(rng, dims, width, most, cuts=(), dtype=jnp.bfloat16):
    drawn = jax.random.normal(rng, dims, jnp.float32) * width
    if len(cuts) > 0:
        drawn = shard_levels(rng, dims, cuts, -0.22, 0.18) * drawn
    return jnp.clip(drawn, min=-most, max=most).astype(dtype)


def setup_inputs(seed: int = 0) -> dict:
    keys = jax.random.split(jax.random.key(seed), 5)
    return {
        "saved_input": bell_draw(keys[0], (BATCH, CHANNELS, SEQ), 1.0, 6.0, ((0, 16), (2, 16))),
        "out_gate": bell_draw(keys[1], (BATCH, CHANNELS, SEQ), 1.0, 6.0, ((0, 16), (2, 16))),
        "grad_out": bell_draw(keys[2], (BATCH, CHANNELS, SEQ), 1.0, 6.0, ((0, 16), (2, 16))),
        "long_filter": bell_draw(keys[3], (CHANNELS, SEQ), SEQ ** -0.5, 0.125, ((0, 16),), jnp.float32),
    }


def reference(saved_input, out_gate, grad_out, long_filter):
    points = 2 * SEQ
    taps_spec = jnp.fft.fft(long_filter.astype(jnp.float32), n=points, axis=-1)

    def per_sequence(running, pieces):
        input_piece, gate_piece, upper_piece = pieces
        conv_grad = (gate_piece.astype(jnp.float32) * upper_piece.astype(jnp.float32)).astype(jnp.bfloat16)
        conv_grad = lax.optimization_barrier(conv_grad)
        input_spec = jnp.fft.fft(input_piece.astype(jnp.float32), n=points, axis=-1)
        grad_spec = jnp.fft.fft(conv_grad.astype(jnp.float32), n=points, axis=-1)
        back_part = jnp.real(jnp.fft.ifft(jnp.conj(taps_spec) * grad_spec, axis=-1))[:, :SEQ]
        cross_part = jnp.real(jnp.fft.ifft(grad_spec * jnp.conj(input_spec), axis=-1))[:, :SEQ]
        return (running + cross_part, back_part.astype(jnp.bfloat16))
    running = jnp.zeros((CHANNELS, SEQ), jnp.float32)
    running, grad_input = lax.scan(per_sequence, running, (saved_input, out_gate, grad_out))
    grad_filter = running * (1.0 / math.sqrt(BATCH * SEQ))
    return (grad_input, grad_filter)
```

```python
import math

import jax
import jax.numpy as jnp
import numpy as np
from jax import lax
from jax.experimental import pallas as pl
from jax.experimental.pallas import tpu as pltpu
from jax.sharding import PartitionSpec as P

MESH = pl.DeviceIdType.MESH
LANES = 128
ROWS = 16
CHUNKS = 4
F32 = jnp.float32
BF16 = jnp.bfloat16


def twiddled_tables():
    k = np.arange(ROWS)[:, None, None]
    n = np.arange(LANES)[None, :, None]
    m = np.arange(LANES)[None, None, :]
    points = 2 * ROWS * LANES
    turns = (n * (2 * (k + 2 * ROWS * m) + 1)) % (2 * points)
    angle = turns * (math.pi / points)
    cos, sin = np.cos(angle), np.sin(angle)
    ahead = np.concatenate(
        [np.concatenate([cos, -sin], axis=2), np.concatenate([sin, cos], axis=2)], axis=1
    )
    return ahead.astype(BF16), np.swapaxes(ahead, 1, 2).astype(BF16)


def split_rows(rows):
    count = len(rows)
    if count == 2:
        turned = rows[1] * math.cos(math.pi / 4)
        return [(rows[0] + turned, -turned), (rows[0] - turned, -turned)]
    even, odd = split_rows(rows[0::2]), split_rows(rows[1::2])
    out = [None] * count
    for k in range(count // 2):
        angle = math.pi * (2 * k + 1) / (2 * count)
        wr, wi = math.cos(angle), -math.sin(angle)
        (er, ei), (pr, pi) = even[k], odd[k]
        tr, ti = wr * pr - wi * pi, wr * pi + wi * pr
        out[k] = (er + tr, ei + ti)
        out[count - 1 - k] = (er - tr, ti - ei)
    return out


def merge_rows(spec):
    count = len(spec)
    if count == 2:
        (a, b), (c, d) = spec
        return [a + c, (a - c - b - d) * math.cos(math.pi / 4)]
    even, odd = [], []
    for k in range(count // 2):
        angle = math.pi * (2 * k + 1) / (2 * count)
        wr, wi = math.cos(angle), -math.sin(angle)
        (pr, pi), (qr, qi) = spec[k], spec[count - 1 - k]
        dr, di = pr - qr, pi + qi
        even.append((pr + qr, pi - qi))
        odd.append((wr * dr + wi * di, wr * di - wi * dr))
    out = [None] * count
    out[0::2], out[1::2] = merge_rows(even), merge_rows(odd)
    return out


def kernel(
    scale,
    u_ref, a_ref, b_ref, h_ref, ahead_ref, back_ref,
    y_ref, f_ref,
    a_buf, b_buf, g_buf, h_buf, u_recv, g_recv, h_first, h_spec, first, last, y_buf,
    f_buf, f_recv1, f_send2, f_recv2, f_send3, f_recv3,
    local_sem, u_send, u_sem, g_send, g_sem, y_send, y_sem,
    s1, r1, s2, r2, s3, r3,
):
    own = f_ref.shape[0]
    size = own // CHUNKS
    dp, me = lax.axis_index("dp"), lax.axis_index("ctx")
    core, z_hi, x = dp % 2, (dp // 2) % 2, dp // 4

    def at_x(step):
        return ((x ^ step) * 4 + z_hi * 2 + core, me)

    other_core = (dp + 1 - 2 * core, me)
    other_z = (dp + 2 - 4 * z_hi, me)

    loads = [
        pltpu.make_async_copy(a_ref, a_buf, local_sem.at[0]),
        pltpu.make_async_copy(b_ref, b_buf, local_sem.at[1]),
        pltpu.make_async_copy(h_ref, h_buf, local_sem.at[2]),
        pltpu.make_async_copy(u_ref.at[pl.ds(me * own, own)], u_recv.at[me], local_sem.at[3]),
    ]
    for copy in loads:
        copy.start()

    barrier = pltpu.get_barrier_semaphore()

    @pl.loop(1, ROWS)
    def _(step):
        pl.semaphore_signal(barrier, inc=1, device_id=(dp, me ^ step), device_id_type=MESH)

    for peer in [other_core, other_z] + [at_x(step) for step in (1, 2, 3)]:
        pl.semaphore_signal(barrier, inc=1, device_id=peer, device_id_type=MESH)

    loads[0].wait()
    loads[1].wait()

    @pl.loop(0, ROWS)
    def _(at):
        rows = pl.ds(at * own, own)
        g_buf[rows] = (a_buf[rows].astype(F32) * b_buf[rows].astype(F32)).astype(BF16)

    keep_g = pltpu.make_async_copy(g_buf.at[pl.ds(me * own, own)], g_recv.at[me], local_sem.at[4])
    keep_g.start()
    pl.semaphore_wait(barrier, ROWS - 1 + 5)

    def exchange(src, dst, send, recv, chunk, step):
        return pltpu.make_async_remote_copy(
            src_ref=src.at[pl.ds((me ^ step) * own + chunk * size, size)],
            dst_ref=dst.at[me, pl.ds(chunk * size, size)],
            send_sem=send.at[chunk, step],
            recv_sem=recv.at[chunk, step],
            device_id=(dp, me ^ step),
            device_id_type=MESH,
        )

    def move_u(chunk, step):
        return exchange(u_ref, u_recv, u_send, u_sem, chunk, step)

    def move_g(chunk, step):
        return exchange(g_buf, g_recv, g_send, g_sem, chunk, step)

    def move_y(chunk, step):
        return pltpu.make_async_remote_copy(
            src_ref=y_buf.at[me ^ step, pl.ds(chunk * size, size)],
            dst_ref=y_ref.at[pl.ds(me * own + chunk * size, size)],
            send_sem=y_send.at[chunk, step],
            recv_sem=y_sem.at[chunk, step],
            device_id=(dp, me ^ step),
            device_id_type=MESH,
        )

    @pl.loop(0, CHUNKS)
    def _(chunk):
        @pl.loop(1, ROWS)
        def _(step):
            move_g(chunk, step).start()
            move_u(chunk, step).start()

    loads[2].wait()

    @pl.loop(0, own // 8)
    def _(at):
        rows = pl.ds(at * 8, 8)
        spec = split_rows([h_buf[rows, j * LANES : (j + 1) * LANES] for j in range(ROWS)])
        for k, (re, im) in enumerate(spec):
            h_first[k, rows, :LANES] = re
            h_first[k, rows, LANES:] = im

    @pl.loop(0, ROWS)
    def _(k):
        h_spec[k] = jnp.dot(
            h_first[k].astype(BF16), ahead_ref[k], preferred_element_type=F32
        ) * (1.0 / (ROWS * LANES))

    loads[3].wait()
    keep_g.wait()

    def compute(chunk):
        base = chunk * size

        @pl.loop(0, size // 16)
        def _(at):
            rows = pl.ds(base + at * 16, 16)
            for place, source in enumerate((g_recv, u_recv)):
                spec = split_rows([source[j, rows].astype(F32) for j in range(ROWS)])
                put = pl.ds(place * size + at * 16, 16)
                for k, (re, im) in enumerate(spec):
                    first[k, put, :LANES] = re.astype(BF16)
                    first[k, put, LANES:] = im.astype(BF16)

        @pl.loop(0, ROWS, unroll=2)
        def _(k):
            spec = jnp.dot(first[k], ahead_ref[k], preferred_element_type=F32)
            gr, gi = spec[:size, :LANES], spec[:size, LANES:]
            ur, ui = spec[size:, :LANES], spec[size:, LANES:]
            hr = h_spec[k, pl.ds(base, size), :LANES]
            hi = h_spec[k, pl.ds(base, size), LANES:]
            to_input = jnp.concatenate([hr * gr + hi * gi, hr * gi - hi * gr], axis=1)
            to_filter = jnp.concatenate([gr * ur + gi * ui, gi * ur - gr * ui], axis=1)
            both = jnp.concatenate([to_input, to_filter], axis=0).astype(BF16)
            last[k] = jnp.dot(both, back_ref[k], preferred_element_type=F32)

        @pl.loop(0, size // 16)
        def _(at):
            rows = pl.ds(base + at * 16, 16)
            for place in range(2):
                take = pl.ds(place * size + at * 16, 16)
                out = merge_rows([(last[k, take, :LANES], last[k, take, LANES:]) for k in range(ROWS)])
                for j in range(ROWS):
                    if place == 0:
                        y_buf[j, rows] = out[j].astype(BF16)
                    else:
                        f_buf[chunk, j % 2, j // 2, pl.ds(at * 16, 16)] = out[j]

    def sum_cores(chunk):
        return pltpu.make_async_remote_copy(
            src_ref=f_buf.at[chunk, 1 - core], dst_ref=f_recv1.at[chunk],
            send_sem=s1.at[chunk], recv_sem=r1.at[chunk],
            device_id=other_core, device_id_type=MESH,
        )

    def sum_x(chunk, step):
        return pltpu.make_async_remote_copy(
            src_ref=f_send2.at[chunk, x ^ step], dst_ref=f_recv2.at[chunk, step],
            send_sem=s2.at[chunk, step], recv_sem=r2.at[chunk, step],
            device_id=at_x(step), device_id_type=MESH,
        )

    def sum_z(chunk):
        return pltpu.make_async_remote_copy(
            src_ref=f_send3.at[chunk], dst_ref=f_recv3.at[chunk],
            send_sem=s3.at[chunk], recv_sem=r3.at[chunk],
            device_id=other_z, device_id_type=MESH,
        )

    def after_cores(chunk):
        sum_cores(chunk).wait()
        for place in range(4):
            for half in range(2):
                at = place * 2 + half
                total = f_buf[chunk, core, at] + f_recv1[chunk, at]
                f_send2[chunk, place, half] = total.astype(BF16)
        for step in (2, 1, 3):
            sum_x(chunk, step).start()

    def held(chunk, half):
        total = f_buf[chunk, core, x * 2 + half] + f_recv1[chunk, x * 2 + half]
        for step in (1, 2, 3):
            total = total + f_recv2[chunk, step, half].astype(F32)
        return total

    def after_x(chunk):
        for step in (1, 2, 3):
            sum_x(chunk, step).wait()
        f_send3[chunk] = held(chunk, 1 - z_hi).astype(BF16)
        sum_z(chunk).start()

    def after_z(chunk):
        sum_z(chunk).wait()
        f_ref[chunk * size : (chunk + 1) * size] = (
            held(chunk, z_hi) + f_recv3[chunk].astype(F32)
        ) * scale

    keeps = []
    for chunk in range(CHUNKS):
        @pl.loop(1, ROWS)
        def _(step):
            move_g(chunk, step).wait_recv()
            move_u(chunk, step).wait_recv()

        compute(chunk)
        sum_cores(chunk).start()

        @pl.loop(1, ROWS)
        def _(step):
            move_y(chunk, step).start()

        keep_y = pltpu.make_async_copy(
            y_buf.at[me, pl.ds(chunk * size, size)],
            y_ref.at[pl.ds(me * own + chunk * size, size)],
            local_sem.at[5 + chunk],
        )
        keep_y.start()
        keeps.append(keep_y)
        if chunk >= 1:
            after_cores(chunk - 1)
        if chunk >= 2:
            after_x(chunk - 2)
        if chunk >= 3:
            after_z(chunk - 3)
    after_cores(CHUNKS - 1)
    after_x(CHUNKS - 2)
    after_x(CHUNKS - 1)
    for chunk in range(CHUNKS - 3, CHUNKS):
        after_z(chunk)

    for keep_y in keeps:
        keep_y.wait()

    @pl.loop(0, CHUNKS)
    def _(chunk):
        @pl.loop(1, ROWS)
        def _(step):
            move_g(chunk, step).wait_send()
            move_u(chunk, step).wait_send()
            move_y(chunk, step).wait()


def on_device(saved_input, out_gate, grad_out, long_filter):
    _, channels, width = saved_input.shape
    own, length = long_filter.shape
    size = own // CHUNKS
    scale = 1.0 / (math.sqrt(lax.axis_size("dp") * length) * ROWS * LANES)
    ahead, back = twiddled_tables()
    in_hbm = pl.BlockSpec(memory_space=pl.ANY)
    in_vmem = pl.BlockSpec(memory_space=pltpu.VMEM)
    dma = pltpu.SemaphoreType.DMA

    def run(*operands):
        return pl.pallas_call(
            lambda *refs: kernel(scale, *refs),
            out_shape=(
                jax.ShapeDtypeStruct((channels, width), BF16),
                jax.ShapeDtypeStruct((own, width), F32),
            ),
            in_specs=[in_hbm] * 4 + [in_vmem] * 2,
            out_specs=(in_hbm, in_vmem),
            scratch_shapes=[
                pltpu.VMEM((channels, width), BF16),
                pltpu.VMEM((channels, width), BF16),
                pltpu.VMEM((channels, width), BF16),
                pltpu.VMEM((own, length), F32),
                pltpu.VMEM((ROWS, own, width), BF16),
                pltpu.VMEM((ROWS, own, width), BF16),
                pltpu.VMEM((ROWS, own, 2 * LANES), F32),
                pltpu.VMEM((ROWS, own, 2 * LANES), F32),
                pltpu.VMEM((ROWS, 2 * size, 2 * LANES), BF16),
                pltpu.VMEM((ROWS, 2 * size, 2 * LANES), F32),
                pltpu.VMEM((ROWS, own, width), BF16),
                pltpu.VMEM((CHUNKS, 2, ROWS // 2, size, LANES), F32),
                pltpu.VMEM((CHUNKS, ROWS // 2, size, LANES), F32),
                pltpu.VMEM((CHUNKS, 4, 2, size, LANES), BF16),
                pltpu.VMEM((CHUNKS, 4, 2, size, LANES), BF16),
                pltpu.VMEM((CHUNKS, size, LANES), BF16),
                pltpu.VMEM((CHUNKS, size, LANES), BF16),
                dma((5 + CHUNKS,)),
                dma((CHUNKS, ROWS)), dma((CHUNKS, ROWS)),
                dma((CHUNKS, ROWS)), dma((CHUNKS, ROWS)),
                dma((CHUNKS, ROWS)), dma((CHUNKS, ROWS)),
                dma((CHUNKS,)), dma((CHUNKS,)),
                dma((CHUNKS, 4)), dma((CHUNKS, 4)),
                dma((CHUNKS,)), dma((CHUNKS,)),
            ],
            compiler_params=pltpu.CompilerParams(
                collective_id=0, has_side_effects=True, vmem_limit_bytes=56 * 2**20
            ),
        )(*operands)

    grad_input, grad_filter = run(
        saved_input[0], out_gate[0], grad_out[0], long_filter, jnp.asarray(ahead), jnp.asarray(back)
    )
    return grad_input[None], grad_filter


def solution(mesh):
    in_specs = (P("dp", None, "ctx"), P("dp", None, "ctx"), P("dp", None, "ctx"), P("ctx", None))
    out_specs = (P("dp", None, "ctx"), P("ctx", "dp"))
    return jax.shard_map(
        on_device, mesh=mesh, in_specs=in_specs, out_specs=out_specs, check_vma=False
    )
```

```python
import math

import jax
import jax.numpy as jnp
import numpy as np
from jax import lax
from jax.experimental import pallas as pl
from jax.experimental.pallas import tpu as pltpu
from jax.sharding import PartitionSpec as P

MESH = pl.DeviceIdType.MESH
LANES = 128
ROWS = 16
HALF = 128
MATE, OWN, SLOTS = HALF, 2 * HALF, 3 * HALF
PARTS = (("own", OWN, 128), ("mate", MATE, 128), ("all", 0, 64), ("all", 64, 64))
COUNT = len(PARTS)
MOST = max(size for _, _, size in PARTS)
PIECES = 8
F32 = jnp.float32
BF16 = jnp.bfloat16


def twiddled_tables():
    k = np.arange(ROWS)[:, None, None]
    n = np.arange(LANES)[None, :, None]
    m = np.arange(LANES)[None, None, :]
    points = 2 * ROWS * LANES
    turns = (n * (2 * (k + 2 * ROWS * m) + 1)) % (2 * points)
    angle = turns * (math.pi / points)
    cos, sin = np.cos(angle), np.sin(angle)
    ahead = np.concatenate(
        [np.concatenate([cos, -sin], axis=2), np.concatenate([sin, cos], axis=2)], axis=1
    )
    return ahead.astype(BF16), np.swapaxes(ahead, 1, 2).astype(BF16)


def split_rows(rows):
    count = len(rows)
    if count == 2:
        turned = rows[1] * math.cos(math.pi / 4)
        return [(rows[0] + turned, -turned), (rows[0] - turned, -turned)]
    even, odd = split_rows(rows[0::2]), split_rows(rows[1::2])
    out = [None] * count
    for k in range(count // 2):
        angle = math.pi * (2 * k + 1) / (2 * count)
        wr, wi = math.cos(angle), -math.sin(angle)
        (er, ei), (pr, pi) = even[k], odd[k]
        tr, ti = wr * pr - wi * pi, wr * pi + wi * pr
        out[k] = (er + tr, ei + ti)
        out[count - 1 - k] = (er - tr, ti - ei)
    return out


def merge_rows(spec):
    count = len(spec)
    if count == 2:
        (a, b), (c, d) = spec
        return [a + c, (a - c - b - d) * math.cos(math.pi / 4)]
    even, odd = [], []
    for k in range(count // 2):
        angle = math.pi * (2 * k + 1) / (2 * count)
        wr, wi = math.cos(angle), -math.sin(angle)
        (pr, pi), (qr, qi) = spec[k], spec[count - 1 - k]
        dr, di = pr - qr, pi + qi
        even.append((pr + qr, pi - qi))
        odd.append((wr * dr + wi * di, wr * di - wi * dr))
    out = [None] * count
    out[0::2], out[1::2] = merge_rows(even), merge_rows(odd)
    return out


def kernel(
    scale,
    u_ref, a_ref, b_ref, h_ref, ahead_ref, back_ref,
    y_ref, f_ref,
    a_buf, b_buf, g_buf, h_buf, h_piece, h_mate, u_recv, g_recv, h_first, h_spec, first, last, y_buf,
    f_buf, f_recv, f_give, f_take, f_send, f_last,
    local_sem, h_send, h_sem, u_send, u_sem, g_send, g_sem, y_send, y_sem,
    s1, r1, s2, r2, s3, r3,
):
    own = f_ref.shape[0]
    dp, me = lax.axis_index("dp"), lax.axis_index("ctx")
    core, z_hi, x = dp % 2, (dp // 2) % 2, dp // 4
    side = (me // 2) % 2
    piece = x * 2 + core

    def cousin(step):
        return ((x ^ (step // 2)) * 4 + z_hi * 2 + (core ^ (step % 2)), me)

    other_z = (dp + 2 - 4 * z_hi, me)
    across = (dp + 2 - 4 * z_hi, me ^ 2)

    def each_step(run):
        @pl.loop(1, ROWS)
        def _(step):
            run(step)

    def near_step(run):
        @pl.loop(1, ROWS // 2)
        def _(at):
            run((at // 2) * 4 + at % 2)

    barrier = pltpu.get_barrier_semaphore()

    def greet(peer):
        pl.semaphore_signal(barrier, inc=1, device_id=peer, device_id_type=MESH)

    each_step(lambda step: greet((dp, me ^ step)))
    for peer in [other_z, across] + [cousin(step) for step in range(1, PIECES)]:
        greet(peer)

    def kept(name, size, base):
        owner = me ^ 2 if name == "mate" else me
        return pl.ds(owner * own + base, size)

    def base_of(name, slot):
        return slot - OWN + HALF if name == "own" else slot

    height = HALF // PIECES
    load_piece = pltpu.make_async_copy(
        h_ref.at[pl.ds(HALF + piece * height, height)], h_piece, local_sem.at[3 + 3 * COUNT]
    )
    load_piece.start()
    loads = [
        pltpu.make_async_copy(a_ref, a_buf, local_sem.at[0]),
        pltpu.make_async_copy(b_ref, b_buf, local_sem.at[1]),
        pltpu.make_async_copy(h_ref, h_buf, local_sem.at[2]),
    ]
    keep_u = [
        pltpu.make_async_copy(
            u_ref.at[kept(name, size, base_of(name, slot))],
            u_recv.at[me, pl.ds(slot, size)],
            local_sem.at[3 + part],
        )
        for part, (name, slot, size) in enumerate(PARTS)
    ]
    for copy in loads + keep_u:
        copy.start()
    pl.semaphore_wait(barrier, ROWS - 1 + 2 + PIECES - 1)

    def exchange(src, dst, send, recv, part, step):
        name, slot, size = PARTS[part]
        owner = me ^ step ^ 2 if name == "mate" else me ^ step
        return pltpu.make_async_remote_copy(
            src_ref=src.at[pl.ds(owner * own + base_of(name, slot), size)],
            dst_ref=dst.at[me, pl.ds(slot, size)],
            send_sem=send.at[part, step],
            recv_sem=recv.at[part, step],
            device_id=(dp, me ^ step),
            device_id_type=MESH,
        )

    def move_u(part, step):
        return exchange(u_ref, u_recv, u_send, u_sem, part, step)

    def move_g(part, step):
        return exchange(g_buf, g_recv, g_send, g_sem, part, step)

    def move_y(part, step):
        name, slot, size = PARTS[part]
        return pltpu.make_async_remote_copy(
            src_ref=y_buf.at[me ^ step, pl.ds(slot, size)],
            dst_ref=y_ref.at[kept(name, size, base_of(name, slot))],
            send_sem=y_send.at[part, step],
            recv_sem=y_sem.at[part, step],
            device_id=(dp, me ^ step),
            device_id_type=MESH,
        )

    def steps_of(part):
        return each_step if PARTS[part][0] == "all" else near_step

    load_piece.wait()
    for j in range(ROWS):
        lanes = slice(j * LANES, (j + 1) * LANES)
        h_mate[1, :height, lanes] = h_piece[:, lanes].astype(BF16)

    give_h = pltpu.make_async_remote_copy(
        src_ref=h_mate.at[1, pl.ds(0, height)],
        dst_ref=h_mate.at[0, pl.ds(piece * height, height)],
        send_sem=h_send.at[0], recv_sem=h_sem.at[0],
        device_id=across, device_id_type=MESH,
    )
    give_h.start()

    def share_h(step):
        rows = pl.ds(piece * height, height)
        return pltpu.make_async_remote_copy(
            src_ref=h_mate.at[0, rows], dst_ref=h_mate.at[0, rows],
            send_sem=h_send.at[step], recv_sem=h_sem.at[step],
            device_id=cousin(step), device_id_type=MESH,
        )

    near_step(lambda step: move_u(0, step).start())
    loads[0].wait()
    loads[1].wait()

    def make_g(begin, size):
        rows = pl.ds(begin, size)
        g_buf[rows] = (a_buf[rows].astype(F32) * b_buf[rows].astype(F32)).astype(BF16)

    def first_g(step):
        make_g((me ^ step) * own + HALF, own - HALF)
        move_g(0, step).start()
    each_step(first_g)
    make_g(me * own + HALF, own - HALF)

    def send_part(part, also=None):
        @pl.loop(0, ROWS // 2)
        def _(at):
            step = (at // 2) * 4 + at % 2
            move_g(part, step + 2).start()
            if PARTS[part][0] == "all":
                move_u(part, step + 2).start()

            @pl.when(at > 0)
            def _():
                move_u(part, step).start()
                move_g(part, step).start()
                if also is not None:
                    move_y(also, step).start()

    give_h.wait_recv()
    for step in range(1, PIECES):
        share_h(step).start()
    send_part(1)

    @pl.loop(0, ROWS)
    def _(to):
        make_g(to * own, HALF)
    send_part(2)
    keep_g = [
        pltpu.make_async_copy(
            g_buf.at[kept(name, size, base_of(name, slot))],
            g_recv.at[me, pl.ds(slot, size)],
            local_sem.at[3 + COUNT + part],
        )
        for part, (name, slot, size) in enumerate(PARTS)
    ]
    for copy in keep_g:
        copy.start()

    @pl.loop(0, ROWS // 2)
    def _(at):
        u_recv[(at // 2) * 4 + 2 * (1 - side) + at % 2, HALF:] = jnp.zeros((SLOTS - HALF, LANES), BF16)

    loads[2].wait()
    @pl.loop(0, own // 16)
    def _(at):
        rows = pl.ds(at * 16, 16)
        put = pl.ds(at * 16 + (at // (HALF // 16)) * HALF, 16)
        spec = split_rows([h_buf[rows, j * LANES : (j + 1) * LANES] for j in range(ROWS)])
        for k, (re, im) in enumerate(spec):
            h_first[k, put, :LANES] = re.astype(BF16)
            h_first[k, put, LANES:] = im.astype(BF16)

    def spectrum(begin, size):
        @pl.loop(0, ROWS)
        def _(k):
            rows = pl.ds(begin, size)
            h_spec[k, rows] = jnp.dot(
                h_first[k, rows], ahead_ref[k], preferred_element_type=F32
            ) * (1.0 / (ROWS * LANES))

    spectrum(0, HALF)
    spectrum(OWN, HALF)

    def mate_taps():
        for step in range(1, PIECES):
            share_h(step).wait_recv()

        @pl.loop(0, HALF // 16)
        def _(at):
            rows = pl.ds(at * 16, 16)
            put = pl.ds(MATE + at * 16, 16)
            spec = split_rows(
                [h_mate[0, rows, j * LANES : (j + 1) * LANES].astype(F32) for j in range(ROWS)]
            )
            for k, (re, im) in enumerate(spec):
                h_first[k, put, :LANES] = re.astype(BF16)
                h_first[k, put, LANES:] = im.astype(BF16)
        spectrum(MATE, HALF)

    def compute(part):
        name, base, size = PARTS[part]

        @pl.loop(0, size // 16)
        def _(at):
            rows = pl.ds(base + at * 16, 16)
            for place, source in enumerate((g_recv, u_recv)):
                spec = split_rows([source[j, rows].astype(F32) for j in range(ROWS)])
                put = pl.ds(place * size + at * 16, 16)
                for k, (re, im) in enumerate(spec):
                    first[k, put, :LANES] = re.astype(BF16)
                    first[k, put, LANES:] = im.astype(BF16)

        @pl.loop(0, ROWS, unroll=2)
        def _(k):
            spec = jnp.dot(first[k, : 2 * size], ahead_ref[k], preferred_element_type=F32)
            gr, gi = spec[:size, :LANES], spec[:size, LANES:]
            ur, ui = spec[size:, :LANES], spec[size:, LANES:]
            hr = h_spec[k, pl.ds(base, size), :LANES]
            hi = h_spec[k, pl.ds(base, size), LANES:]
            to_input = jnp.concatenate([hr * gr + hi * gi, hr * gi - hi * gr], axis=1)
            to_filter = jnp.concatenate([gr * ur + gi * ui, gi * ur - gr * ui], axis=1)
            both = jnp.concatenate([to_input, to_filter], axis=0).astype(BF16)
            last[k, : 2 * size] = jnp.dot(both, back_ref[k], preferred_element_type=F32)

        @pl.loop(0, size // 16)
        def _(at):
            rows = pl.ds(base + at * 16, 16)
            for place in range(2):
                take = pl.ds(place * size + at * 16, 16)
                out = merge_rows([(last[k, take, :LANES], last[k, take, LANES:]) for k in range(ROWS)])
                for j in range(ROWS):
                    if place == 0:
                        y_buf[j, rows] = out[j].astype(BF16)
                    else:
                        f_buf[(j // 4) * 2 + j % 2, (j // 2) % 2, rows] = out[j].astype(BF16)

    def slots(part):
        return pl.ds(PARTS[part][1], PARTS[part][2])

    def sum_cousins(part, step):
        return pltpu.make_async_remote_copy(
            src_ref=f_buf.at[piece ^ step, :, slots(part)],
            dst_ref=f_recv.at[step, :, slots(part)],
            send_sem=s1.at[part, step], recv_sem=r1.at[part, step],
            device_id=cousin(step), device_id_type=MESH,
        )

    sum_mate = pltpu.make_async_remote_copy(
        src_ref=f_give, dst_ref=f_take, send_sem=s2, recv_sem=r2,
        device_id=across, device_id_type=MESH,
    )

    def sum_z(part):
        return pltpu.make_async_remote_copy(
            src_ref=f_send.at[slots(part)], dst_ref=f_last.at[slots(part)],
            send_sem=s3.at[part], recv_sem=r3.at[part],
            device_id=other_z, device_id_type=MESH,
        )

    def held(part, half):
        name, slot, size = PARTS[part]
        total = f_buf[piece, half, slots(part)].astype(F32)
        for step in range(1, PIECES):
            total = total + f_recv[step, half, slots(part)].astype(F32)
        if name == "own":
            total = total + f_take[half].astype(F32)
        return total

    def after_cousins(part):
        for step in range(1, PIECES):
            sum_cousins(part, step).wait()
        name = PARTS[part][0]
        if name == "mate":
            for half in range(2):
                f_give[half] = held(part, half).astype(BF16)
            sum_mate.start()
        else:
            if name == "own":
                sum_mate.wait()
            f_send[slots(part)] = held(part, 1 - z_hi).astype(BF16)
            sum_z(part).start()

    def after_z(part):
        name, slot, size = PARTS[part]
        sum_z(part).wait()
        f_ref[pl.ds(base_of(name, slot), size)] = (
            held(part, z_hi) + f_last[slots(part)].astype(F32)
        ) * scale

    def keep_y(part):
        name, slot, size = PARTS[part]
        return pltpu.make_async_copy(
            y_buf.at[me, pl.ds(slot, size)],
            y_ref.at[kept(name, size, base_of(name, slot))],
            local_sem.at[3 + 2 * COUNT + part],
        )

    def begin(part):
        each_step(lambda step: move_g(part, step).wait_recv())
        steps_of(part)(lambda step: move_u(part, step).wait_recv())
        keep_g[part].wait()
        keep_u[part].wait()
        if PARTS[part][0] == "mate":
            mate_taps()
        compute(part)
        for step in range(1, PIECES):
            sum_cousins(part, step).start()
        keep_y(part).start()

    begin(0)
    send_part(3, also=0)
    begin(1)
    begin(2)
    each_step(lambda step: move_y(2, step).start())
    near_step(lambda step: move_y(1, step).start())
    after_cousins(1)
    begin(3)
    each_step(lambda step: move_y(3, step).start())
    after_cousins(0)
    after_cousins(2)
    after_cousins(3)
    after_z(0)
    after_z(2)
    after_z(3)

    give_h.wait_send()
    for step in range(1, PIECES):
        share_h(step).wait_send()
    for part in range(COUNT):
        keep_y(part).wait()
        each_step(lambda step: move_g(part, step).wait_send())

        def finish(step):
            move_u(part, step).wait_send()
            move_y(part, step).wait()
        steps_of(part)(finish)


def on_device(saved_input, out_gate, grad_out, long_filter):
    _, channels, width = saved_input.shape
    own, length = long_filter.shape
    scale = 1.0 / (math.sqrt(lax.axis_size("dp") * length) * ROWS * LANES)
    ahead, back = twiddled_tables()
    in_hbm = pl.BlockSpec(memory_space=pl.ANY)
    in_vmem = pl.BlockSpec(memory_space=pltpu.VMEM)
    dma = pltpu.SemaphoreType.DMA

    def run(*operands):
        return pl.pallas_call(
            lambda *refs: kernel(scale, *refs),
            out_shape=(
                jax.ShapeDtypeStruct((channels, width), BF16),
                jax.ShapeDtypeStruct((own, width), F32),
            ),
            in_specs=[in_hbm] * 4 + [in_vmem] * 2,
            out_specs=(in_hbm, in_vmem),
            scratch_shapes=[
                pltpu.VMEM((channels, width), BF16),
                pltpu.VMEM((channels, width), BF16),
                pltpu.VMEM((channels, width), BF16),
                pltpu.VMEM((own, length), F32),
                pltpu.VMEM((HALF // PIECES, length), F32),
                pltpu.VMEM((2, HALF, length), BF16),
                pltpu.VMEM((ROWS, SLOTS, width), BF16),
                pltpu.VMEM((ROWS, SLOTS, width), BF16),
                pltpu.VMEM((ROWS, SLOTS, 2 * LANES), BF16),
                pltpu.VMEM((ROWS, SLOTS, 2 * LANES), F32),
                pltpu.VMEM((ROWS, 2 * MOST, 2 * LANES), BF16),
                pltpu.VMEM((ROWS, 2 * MOST, 2 * LANES), F32),
                pltpu.VMEM((ROWS, SLOTS, width), BF16),
                pltpu.VMEM((PIECES, 2, SLOTS, LANES), BF16),
                pltpu.VMEM((PIECES, 2, SLOTS, LANES), BF16),
                pltpu.VMEM((2, HALF, LANES), BF16),
                pltpu.VMEM((2, HALF, LANES), BF16),
                pltpu.VMEM((SLOTS, LANES), BF16),
                pltpu.VMEM((SLOTS, LANES), BF16),
                dma((4 + 3 * COUNT,)),
                dma((PIECES,)), dma((PIECES,)),
                dma((COUNT, ROWS)), dma((COUNT, ROWS)),
                dma((COUNT, ROWS)), dma((COUNT, ROWS)),
                dma((COUNT, ROWS)), dma((COUNT, ROWS)),
                dma((COUNT, PIECES)), dma((COUNT, PIECES)),
                dma, dma,
                dma((COUNT,)), dma((COUNT,)),
            ],
            compiler_params=pltpu.CompilerParams(
                collective_id=0, has_side_effects=True, vmem_limit_bytes=56 * 2**20
            ),
        )(*operands)

    grad_input, grad_filter = run(
        saved_input[0], out_gate[0], grad_out[0], long_filter, jnp.asarray(ahead), jnp.asarray(back)
    )
    return grad_input[None], grad_filter


def solution(mesh):
    in_specs = (P("dp", None, "ctx"), P("dp", None, "ctx"), P("dp", None, "ctx"), P("ctx", None))
    out_specs = (P("dp", None, "ctx"), P("ctx", "dp"))
    return jax.shard_map(
        on_device, mesh=mesh, in_specs=in_specs, out_specs=out_specs, check_vma=False
    )
```

```python
import math

import jax
import jax.numpy as jnp
import numpy as np
from jax import lax
from jax.experimental import pallas as pl
from jax.experimental.pallas import tpu as pltpu
from jax.sharding import PartitionSpec as P

MESH = pl.DeviceIdType.MESH
LANES = 128
ROWS = 16
HALF = 128
MATE, OWN, SLOTS = HALF, 2 * HALF, 3 * HALF
PARTS = (("own", OWN, 128), ("mate", MATE, 128), ("all", 0, 64), ("all", 64, 64))
COUNT = len(PARTS)
MOST = max(size for _, _, size in PARTS)
PIECES = 8
F32 = jnp.float32
BF16 = jnp.bfloat16


def twiddled_tables():
    k = np.arange(ROWS)[:, None, None]
    n = np.arange(LANES)[None, :, None]
    m = np.arange(LANES)[None, None, :]
    points = 2 * ROWS * LANES
    turns = (n * (2 * (k + 2 * ROWS * m) + 1)) % (2 * points)
    angle = turns * (math.pi / points)
    cos, sin = np.cos(angle), np.sin(angle)
    ahead = np.concatenate(
        [np.concatenate([cos, -sin], axis=2), np.concatenate([sin, cos], axis=2)], axis=1
    )
    return ahead.astype(BF16), np.swapaxes(ahead, 1, 2).astype(BF16)


def split_rows(rows):
    count = len(rows)
    if count == 2:
        turned = rows[1] * math.cos(math.pi / 4)
        return [(rows[0] + turned, -turned), (rows[0] - turned, -turned)]
    even, odd = split_rows(rows[0::2]), split_rows(rows[1::2])
    out = [None] * count
    for k in range(count // 2):
        angle = math.pi * (2 * k + 1) / (2 * count)
        wr, wi = math.cos(angle), -math.sin(angle)
        (er, ei), (pr, pi) = even[k], odd[k]
        tr, ti = wr * pr - wi * pi, wr * pi + wi * pr
        out[k] = (er + tr, ei + ti)
        out[count - 1 - k] = (er - tr, ti - ei)
    return out


def merge_rows(spec):
    count = len(spec)
    if count == 2:
        (a, b), (c, d) = spec
        return [a + c, (a - c - b - d) * math.cos(math.pi / 4)]
    even, odd = [], []
    for k in range(count // 2):
        angle = math.pi * (2 * k + 1) / (2 * count)
        wr, wi = math.cos(angle), -math.sin(angle)
        (pr, pi), (qr, qi) = spec[k], spec[count - 1 - k]
        dr, di = pr - qr, pi + qi
        even.append((pr + qr, pi - qi))
        odd.append((wr * dr + wi * di, wr * di - wi * dr))
    out = [None] * count
    out[0::2], out[1::2] = merge_rows(even), merge_rows(odd)
    return out


def kernel(
    scale,
    u_ref, a_ref, b_ref, h_ref, ahead_ref, back_ref,
    y_ref, f_ref,
    a_buf, b_buf, g_buf, h_buf, h_piece, h_mate, u_recv, g_recv, h_first, h_spec, first, last, y_buf,
    f_buf, f_recv, f_give, f_take, f_send, f_last,
    local_sem, h_send, h_sem, u_send, u_sem, g_send, g_sem, y_send, y_sem,
    s1, r1, s2, r2, s3, r3,
):
    own = f_ref.shape[0]
    dp, me = lax.axis_index("dp"), lax.axis_index("ctx")
    core, z_hi, x = dp % 2, (dp // 2) % 2, dp // 4
    side = (me // 2) % 2
    piece = x * 2 + core

    def cousin(step):
        return ((x ^ (step // 2)) * 4 + z_hi * 2 + (core ^ (step % 2)), me)

    other_z = (dp + 2 - 4 * z_hi, me)
    across = (dp + 2 - 4 * z_hi, me ^ 2)

    def each_step(run):
        @pl.loop(1, ROWS)
        def _(step):
            run(step)

    def near_step(run):
        @pl.loop(1, ROWS // 2)
        def _(at):
            run((at // 2) * 4 + at % 2)

    barrier = pltpu.get_barrier_semaphore()

    def greet(peer):
        pl.semaphore_signal(barrier, inc=1, device_id=peer, device_id_type=MESH)

    each_step(lambda step: greet((dp, me ^ step)))
    for peer in [other_z, across] + [cousin(step) for step in range(1, PIECES)]:
        greet(peer)

    def kept(name, size, base):
        owner = me ^ 2 if name == "mate" else me
        return pl.ds(owner * own + base, size)

    def base_of(name, slot):
        return slot - OWN + HALF if name == "own" else slot

    height = HALF // PIECES
    load_piece = pltpu.make_async_copy(
        h_ref.at[pl.ds(HALF + piece * height, height)], h_piece, local_sem.at[3 + 3 * COUNT]
    )
    load_piece.start()
    loads = [
        pltpu.make_async_copy(a_ref, a_buf, local_sem.at[0]),
        pltpu.make_async_copy(b_ref, b_buf, local_sem.at[1]),
        pltpu.make_async_copy(h_ref, h_buf, local_sem.at[2]),
    ]
    keep_u = [
        pltpu.make_async_copy(
            u_ref.at[kept(name, size, base_of(name, slot))],
            u_recv.at[me, pl.ds(slot, size)],
            local_sem.at[3 + part],
        )
        for part, (name, slot, size) in enumerate(PARTS)
    ]
    for copy in loads + keep_u:
        copy.start()
    pl.semaphore_wait(barrier, ROWS - 1 + 2 + PIECES - 1)

    def exchange(src, dst, send, recv, part, step):
        name, slot, size = PARTS[part]
        owner = me ^ step ^ 2 if name == "mate" else me ^ step
        return pltpu.make_async_remote_copy(
            src_ref=src.at[pl.ds(owner * own + base_of(name, slot), size)],
            dst_ref=dst.at[me, pl.ds(slot, size)],
            send_sem=send.at[part],
            recv_sem=recv.at[part],
            device_id=(dp, me ^ step),
            device_id_type=MESH,
        )

    def move_u(part, step):
        return exchange(u_ref, u_recv, u_send, u_sem, part, step)

    def move_g(part, step):
        return exchange(g_buf, g_recv, g_send, g_sem, part, step)

    def move_y(part, step):
        name, slot, size = PARTS[part]
        return pltpu.make_async_remote_copy(
            src_ref=y_buf.at[me ^ step, pl.ds(slot, size)],
            dst_ref=y_ref.at[kept(name, size, base_of(name, slot))],
            send_sem=y_send.at[part],
            recv_sem=y_sem.at[part],
            device_id=(dp, me ^ step),
            device_id_type=MESH,
        )

    def all_of(ref, sem):
        pltpu.make_async_copy(ref, ref, sem).wait()

    def blocks(part, whole=False):
        name, slot, size = PARTS[part]
        count = ROWS - 1 if whole or name == "all" else ROWS // 2 - 1
        return g_recv.at[pl.ds(0, count), pl.ds(slot, size)]

    load_piece.wait()
    for j in range(ROWS):
        lanes = slice(j * LANES, (j + 1) * LANES)
        h_mate[1, :height, lanes] = h_piece[:, lanes].astype(BF16)

    give_h = pltpu.make_async_remote_copy(
        src_ref=h_mate.at[1, pl.ds(0, height)],
        dst_ref=h_mate.at[0, pl.ds(piece * height, height)],
        send_sem=h_send.at[0], recv_sem=h_sem.at[0],
        device_id=across, device_id_type=MESH,
    )
    give_h.start()

    def share_h(step):
        rows = pl.ds(piece * height, height)
        return pltpu.make_async_remote_copy(
            src_ref=h_mate.at[0, rows], dst_ref=h_mate.at[0, rows],
            send_sem=h_send.at[1], recv_sem=h_sem.at[1],
            device_id=cousin(step), device_id_type=MESH,
        )

    near_step(lambda step: move_u(0, step).start())
    loads[0].wait()
    loads[1].wait()

    def make_g(begin, size):
        rows = pl.ds(begin, size)
        g_buf[rows] = (a_buf[rows].astype(F32) * b_buf[rows].astype(F32)).astype(BF16)

    def first_g(step):
        make_g((me ^ step) * own + HALF, own - HALF)
        move_g(0, step).start()
    each_step(first_g)
    make_g(me * own + HALF, own - HALF)

    def send_part(part, also=None):
        @pl.loop(0, ROWS // 2)
        def _(at):
            step = (at // 2) * 4 + at % 2
            move_g(part, step + 2).start()
            if PARTS[part][0] == "all":
                move_u(part, step + 2).start()

            @pl.when(at > 0)
            def _():
                move_u(part, step).start()
                move_g(part, step).start()
                if also is not None:
                    move_y(also, step).start()

    give_h.wait_recv()
    for step in range(1, PIECES):
        share_h(step).start()
    send_part(1)

    @pl.loop(0, ROWS)
    def _(to):
        make_g(to * own, HALF)
    send_part(2)
    keep_g = [
        pltpu.make_async_copy(
            g_buf.at[kept(name, size, base_of(name, slot))],
            g_recv.at[me, pl.ds(slot, size)],
            local_sem.at[3 + COUNT + part],
        )
        for part, (name, slot, size) in enumerate(PARTS)
    ]
    for copy in keep_g:
        copy.start()

    @pl.loop(0, ROWS // 2)
    def _(at):
        u_recv[(at // 2) * 4 + 2 * (1 - side) + at % 2, HALF:] = jnp.zeros((SLOTS - HALF, LANES), BF16)

    loads[2].wait()
    @pl.loop(0, own // 16)
    def _(at):
        rows = pl.ds(at * 16, 16)
        put = pl.ds(at * 16 + (at // (HALF // 16)) * HALF, 16)
        spec = split_rows([h_buf[rows, j * LANES : (j + 1) * LANES] for j in range(ROWS)])
        for k, (re, im) in enumerate(spec):
            h_first[k, put, :LANES] = re.astype(BF16)
            h_first[k, put, LANES:] = im.astype(BF16)

    def spectrum(begin, size):
        @pl.loop(0, ROWS)
        def _(k):
            rows = pl.ds(begin, size)
            h_spec[k, rows] = jnp.dot(
                h_first[k, rows], ahead_ref[k], preferred_element_type=F32
            ) * (1.0 / (ROWS * LANES))

    spectrum(0, HALF)
    spectrum(OWN, HALF)

    def mate_taps():
        all_of(h_mate.at[0, pl.ds(0, (PIECES - 1) * height)], h_sem.at[1])

        @pl.loop(0, HALF // 16)
        def _(at):
            rows = pl.ds(at * 16, 16)
            put = pl.ds(MATE + at * 16, 16)
            spec = split_rows(
                [h_mate[0, rows, j * LANES : (j + 1) * LANES].astype(F32) for j in range(ROWS)]
            )
            for k, (re, im) in enumerate(spec):
                h_first[k, put, :LANES] = re.astype(BF16)
                h_first[k, put, LANES:] = im.astype(BF16)
        spectrum(MATE, HALF)

    def compute(part):
        name, base, size = PARTS[part]

        @pl.loop(0, size // 16)
        def _(at):
            rows = pl.ds(base + at * 16, 16)
            for place, source in enumerate((g_recv, u_recv)):
                spec = split_rows([source[j, rows].astype(F32) for j in range(ROWS)])
                put = pl.ds(place * size + at * 16, 16)
                for k, (re, im) in enumerate(spec):
                    first[k, put, :LANES] = re.astype(BF16)
                    first[k, put, LANES:] = im.astype(BF16)

        @pl.loop(0, ROWS, unroll=2)
        def _(k):
            spec = jnp.dot(first[k, : 2 * size], ahead_ref[k], preferred_element_type=F32)
            gr, gi = spec[:size, :LANES], spec[:size, LANES:]
            ur, ui = spec[size:, :LANES], spec[size:, LANES:]
            hr = h_spec[k, pl.ds(base, size), :LANES]
            hi = h_spec[k, pl.ds(base, size), LANES:]
            to_input = jnp.concatenate([hr * gr + hi * gi, hr * gi - hi * gr], axis=1)
            to_filter = jnp.concatenate([gr * ur + gi * ui, gi * ur - gr * ui], axis=1)
            both = jnp.concatenate([to_input, to_filter], axis=0).astype(BF16)
            last[k, : 2 * size] = jnp.dot(both, back_ref[k], preferred_element_type=F32)

        @pl.loop(0, size // 16)
        def _(at):
            rows = pl.ds(base + at * 16, 16)
            for place in range(2):
                take = pl.ds(place * size + at * 16, 16)
                out = merge_rows([(last[k, take, :LANES], last[k, take, LANES:]) for k in range(ROWS)])
                for j in range(ROWS):
                    if place == 0:
                        y_buf[j, rows] = out[j].astype(BF16)
                    else:
                        f_buf[(j // 4) * 2 + j % 2, (j // 2) % 2, rows] = out[j].astype(BF16)

    def slots(part):
        return pl.ds(PARTS[part][1], PARTS[part][2])

    def sum_cousins(part, step):
        return pltpu.make_async_remote_copy(
            src_ref=f_buf.at[piece ^ step, :, slots(part)],
            dst_ref=f_recv.at[step, :, slots(part)],
            send_sem=s1.at[part], recv_sem=r1.at[part],
            device_id=cousin(step), device_id_type=MESH,
        )

    sum_mate = pltpu.make_async_remote_copy(
        src_ref=f_give, dst_ref=f_take, send_sem=s2, recv_sem=r2,
        device_id=across, device_id_type=MESH,
    )

    def sum_z(part):
        return pltpu.make_async_remote_copy(
            src_ref=f_send.at[slots(part)], dst_ref=f_last.at[slots(part)],
            send_sem=s3.at[part], recv_sem=r3.at[part],
            device_id=other_z, device_id_type=MESH,
        )

    def held(part, half):
        name, slot, size = PARTS[part]
        total = f_buf[piece, half, slots(part)].astype(F32)
        for step in range(1, PIECES):
            total = total + f_recv[step, half, slots(part)].astype(F32)
        if name == "own":
            total = total + f_take[half].astype(F32)
        return total

    def after_cousins(part):
        all_of(f_recv.at[pl.ds(1, PIECES - 1), :, slots(part)], r1.at[part])
        name = PARTS[part][0]
        if name == "mate":
            for half in range(2):
                f_give[half] = held(part, half).astype(BF16)
            sum_mate.start()
        else:
            if name == "own":
                sum_mate.wait()
            f_send[slots(part)] = held(part, 1 - z_hi).astype(BF16)
            sum_z(part).start()

    def after_z(part):
        name, slot, size = PARTS[part]
        sum_z(part).wait()
        f_ref[pl.ds(base_of(name, slot), size)] = (
            held(part, z_hi) + f_last[slots(part)].astype(F32)
        ) * scale

    def keep_y(part):
        name, slot, size = PARTS[part]
        return pltpu.make_async_copy(
            y_buf.at[me, pl.ds(slot, size)],
            y_ref.at[kept(name, size, base_of(name, slot))],
            local_sem.at[3 + 2 * COUNT + part],
        )

    def begin(part):
        all_of(blocks(part, True), g_sem.at[part])
        all_of(blocks(part), u_sem.at[part])
        keep_g[part].wait()
        keep_u[part].wait()
        if PARTS[part][0] == "mate":
            mate_taps()
        compute(part)
        for step in range(1, PIECES):
            sum_cousins(part, step).start()
        keep_y(part).start()

    begin(0)
    send_part(3, also=0)
    begin(1)
    begin(2)
    each_step(lambda step: move_y(2, step).start())
    near_step(lambda step: move_y(1, step).start())
    after_cousins(1)
    begin(3)
    each_step(lambda step: move_y(3, step).start())
    after_cousins(0)
    after_cousins(2)
    after_cousins(3)
    after_z(0)
    after_z(2)
    after_z(3)

    give_h.wait_send()
    all_of(h_mate.at[0, pl.ds(0, (PIECES - 1) * height)], h_send.at[1])
    for part in range(COUNT):
        keep_y(part).wait()
        all_of(f_recv.at[pl.ds(1, PIECES - 1), :, slots(part)], s1.at[part])
        all_of(blocks(part, True), g_send.at[part])
        all_of(blocks(part), u_send.at[part])
        all_of(blocks(part), y_send.at[part])
        all_of(blocks(part), y_sem.at[part])


def on_device(saved_input, out_gate, grad_out, long_filter):
    _, channels, width = saved_input.shape
    own, length = long_filter.shape
    scale = 1.0 / (math.sqrt(lax.axis_size("dp") * length) * ROWS * LANES)
    ahead, back = twiddled_tables()
    in_hbm = pl.BlockSpec(memory_space=pl.ANY)
    in_vmem = pl.BlockSpec(memory_space=pltpu.VMEM)
    dma = pltpu.SemaphoreType.DMA

    def run(*operands):
        return pl.pallas_call(
            lambda *refs: kernel(scale, *refs),
            out_shape=(
                jax.ShapeDtypeStruct((channels, width), BF16),
                jax.ShapeDtypeStruct((own, width), F32),
            ),
            in_specs=[in_hbm] * 4 + [in_vmem] * 2,
            out_specs=(in_hbm, in_vmem),
            scratch_shapes=[
                pltpu.VMEM((channels, width), BF16),
                pltpu.VMEM((channels, width), BF16),
                pltpu.VMEM((channels, width), BF16),
                pltpu.VMEM((own, length), F32),
                pltpu.VMEM((HALF // PIECES, length), F32),
                pltpu.VMEM((2, HALF, length), BF16),
                pltpu.VMEM((ROWS, SLOTS, width), BF16),
                pltpu.VMEM((ROWS, SLOTS, width), BF16),
                pltpu.VMEM((ROWS, SLOTS, 2 * LANES), BF16),
                pltpu.VMEM((ROWS, SLOTS, 2 * LANES), F32),
                pltpu.VMEM((ROWS, 2 * MOST, 2 * LANES), BF16),
                pltpu.VMEM((ROWS, 2 * MOST, 2 * LANES), F32),
                pltpu.VMEM((ROWS, SLOTS, width), BF16),
                pltpu.VMEM((PIECES, 2, SLOTS, LANES), BF16),
                pltpu.VMEM((PIECES, 2, SLOTS, LANES), BF16),
                pltpu.VMEM((2, HALF, LANES), BF16),
                pltpu.VMEM((2, HALF, LANES), BF16),
                pltpu.VMEM((SLOTS, LANES), BF16),
                pltpu.VMEM((SLOTS, LANES), BF16),
                dma((4 + 3 * COUNT,)),
                dma((2,)), dma((2,)),
                dma((COUNT,)), dma((COUNT,)),
                dma((COUNT,)), dma((COUNT,)),
                dma((COUNT,)), dma((COUNT,)),
                dma((COUNT,)), dma((COUNT,)),
                dma, dma,
                dma((COUNT,)), dma((COUNT,)),
            ],
            compiler_params=pltpu.CompilerParams(
                collective_id=0, has_side_effects=True, vmem_limit_bytes=56 * 2**20
            ),
        )(*operands)

    grad_input, grad_filter = run(
        saved_input[0], out_gate[0], grad_out[0], long_filter, jnp.asarray(ahead), jnp.asarray(back)
    )
    return grad_input[None], grad_filter


def solution(mesh):
    in_specs = (P("dp", None, "ctx"), P("dp", None, "ctx"), P("dp", None, "ctx"), P("ctx", None))
    out_specs = (P("dp", None, "ctx"), P("ctx", "dp"))
    return jax.shard_map(
        on_device, mesh=mesh, in_specs=in_specs, out_specs=out_specs, check_vma=False
    )
```

```python
import math

import jax
import jax.numpy as jnp
import numpy as np
from jax import lax
from jax.experimental import pallas as pl
from jax.experimental.pallas import tpu as pltpu
from jax.sharding import PartitionSpec as P

MESH = pl.DeviceIdType.MESH
LANES = 128
ROWS = 16
HALF = 128
MATE, OWN, SLOTS = HALF, 2 * HALF, 3 * HALF
PARTS = (("own", OWN, 128), ("mate", MATE, 128), ("all", 0, 64), ("all", 64, 64))
COUNT = len(PARTS)
MOST = max(size for _, _, size in PARTS)
PIECES = 8
F32 = jnp.float32
BF16 = jnp.bfloat16


def twiddled_tables():
    k = np.arange(ROWS)[:, None, None]
    n = np.arange(LANES)[None, :, None]
    m = np.arange(LANES)[None, None, :]
    points = 2 * ROWS * LANES
    turns = (n * (2 * (k + 2 * ROWS * m) + 1)) % (2 * points)
    angle = turns * (math.pi / points)
    cos, sin = np.cos(angle), np.sin(angle)
    ahead = np.concatenate(
        [np.concatenate([cos, -sin], axis=2), np.concatenate([sin, cos], axis=2)], axis=1
    )
    return ahead.astype(BF16), np.swapaxes(ahead, 1, 2).astype(BF16)


def split_rows(rows):
    count = len(rows)
    if count == 2:
        turned = rows[1] * math.cos(math.pi / 4)
        return [(rows[0] + turned, -turned), (rows[0] - turned, -turned)]
    even, odd = split_rows(rows[0::2]), split_rows(rows[1::2])
    out = [None] * count
    for k in range(count // 2):
        angle = math.pi * (2 * k + 1) / (2 * count)
        wr, wi = math.cos(angle), -math.sin(angle)
        (er, ei), (pr, pi) = even[k], odd[k]
        tr, ti = wr * pr - wi * pi, wr * pi + wi * pr
        out[k] = (er + tr, ei + ti)
        out[count - 1 - k] = (er - tr, ti - ei)
    return out


def merge_rows(spec):
    count = len(spec)
    if count == 2:
        (a, b), (c, d) = spec
        return [a + c, (a - c - b - d) * math.cos(math.pi / 4)]
    even, odd = [], []
    for k in range(count // 2):
        angle = math.pi * (2 * k + 1) / (2 * count)
        wr, wi = math.cos(angle), -math.sin(angle)
        (pr, pi), (qr, qi) = spec[k], spec[count - 1 - k]
        dr, di = pr - qr, pi + qi
        even.append((pr + qr, pi - qi))
        odd.append((wr * dr + wi * di, wr * di - wi * dr))
    out = [None] * count
    out[0::2], out[1::2] = merge_rows(even), merge_rows(odd)
    return out


def kernel(
    scale,
    u_ref, a_ref, b_ref, h_ref, ahead_hbm, back_hbm,
    y_ref, f_ref,
    ahead_ref, back_ref, a_buf, b_buf, g_buf, h_buf, h_piece, h_mate, u_recv, g_recv, h_first, h_spec, first, last, y_buf,
    f_buf, f_recv, f_give, f_take, f_send, f_last,
    local_sem, h_send, h_sem, u_send, u_sem, g_send, g_sem, y_send, y_sem,
    s1, r1, s2, r2, s3, r3,
):
    own = f_ref.shape[0]
    dp, me = lax.axis_index("dp"), lax.axis_index("ctx")
    core, z_hi, x = dp % 2, (dp // 2) % 2, dp // 4
    side = (me // 2) % 2
    piece = x * 2 + core

    def cousin(step):
        return ((x ^ (step // 2)) * 4 + z_hi * 2 + (core ^ (step % 2)), me)

    other_z = (dp + 2 - 4 * z_hi, me)
    across = (dp + 2 - 4 * z_hi, me ^ 2)

    def each_step(run):
        @pl.loop(1, ROWS)
        def _(step):
            run(step)

    def near_step(run):
        @pl.loop(1, ROWS // 2)
        def _(at):
            run((at // 2) * 4 + at % 2)

    barrier = pltpu.get_barrier_semaphore()

    def greet(peer):
        pl.semaphore_signal(barrier, inc=1, device_id=peer, device_id_type=MESH)

    each_step(lambda step: greet((dp, me ^ step)))
    for step in range(1, PIECES):
        greet(cousin(step))

    def kept(name, size, base):
        owner = me ^ 2 if name == "mate" else me
        return pl.ds(owner * own + base, size)

    def base_of(name, slot):
        return slot - OWN + HALF if name == "own" else slot

    height = HALF // PIECES
    load_piece = pltpu.make_async_copy(
        h_ref.at[pl.ds(HALF + piece * height, height)], h_piece, local_sem.at[3 + 3 * COUNT]
    )
    load_piece.start()
    loads = [
        pltpu.make_async_copy(a_ref, a_buf, local_sem.at[0]),
        pltpu.make_async_copy(b_ref, b_buf, local_sem.at[1]),
        pltpu.make_async_copy(h_ref, h_buf, local_sem.at[2]),
        pltpu.make_async_copy(ahead_hbm, ahead_ref, local_sem.at[4 + 3 * COUNT]),
        pltpu.make_async_copy(back_hbm, back_ref, local_sem.at[5 + 3 * COUNT]),
    ]
    keep_u = [
        pltpu.make_async_copy(
            u_ref.at[kept(name, size, base_of(name, slot))],
            u_recv.at[me, pl.ds(slot, size)],
            local_sem.at[3 + part],
        )
        for part, (name, slot, size) in enumerate(PARTS)
    ]
    for copy in loads[:2]:
        copy.start()

    for peer in (other_z, across):
        greet(peer)
    pl.semaphore_wait(barrier, ROWS - 1 + PIECES - 1 + 2)

    def exchange(src, dst, send, recv, part, step):
        name, slot, size = PARTS[part]
        owner = me ^ step ^ 2 if name == "mate" else me ^ step
        return pltpu.make_async_remote_copy(
            src_ref=src.at[pl.ds(owner * own + base_of(name, slot), size)],
            dst_ref=dst.at[me, pl.ds(slot, size)],
            send_sem=send.at[part],
            recv_sem=recv.at[part],
            device_id=(dp, me ^ step),
            device_id_type=MESH,
        )

    def move_u(part, step):
        return exchange(u_ref, u_recv, u_send, u_sem, part, step)

    def move_g(part, step):
        return exchange(g_buf, g_recv, g_send, g_sem, part, step)

    def move_y(part, step):
        name, slot, size = PARTS[part]
        return pltpu.make_async_remote_copy(
            src_ref=y_buf.at[me ^ step, pl.ds(slot, size)],
            dst_ref=y_ref.at[kept(name, size, base_of(name, slot))],
            send_sem=y_send.at[part],
            recv_sem=y_sem.at[part],
            device_id=(dp, me ^ step),
            device_id_type=MESH,
        )

    def all_of(ref, sem):
        pltpu.make_async_copy(ref, ref, sem).wait()

    def blocks(part, whole=False):
        name, slot, size = PARTS[part]
        count = ROWS - 1 if whole or name == "all" else ROWS // 2 - 1
        return g_recv.at[pl.ds(0, count), pl.ds(slot, size)]

    load_piece.wait()
    for j in range(ROWS):
        lanes = slice(j * LANES, (j + 1) * LANES)
        h_mate[1, :height, lanes] = h_piece[:, lanes].astype(BF16)

    give_h = pltpu.make_async_remote_copy(
        src_ref=h_mate.at[1, pl.ds(0, height)],
        dst_ref=h_mate.at[0, pl.ds(piece * height, height)],
        send_sem=h_send.at[0], recv_sem=h_sem.at[0],
        device_id=across, device_id_type=MESH,
    )
    give_h.start()

    def share_h(step):
        rows = pl.ds(piece * height, height)
        return pltpu.make_async_remote_copy(
            src_ref=h_mate.at[0, rows], dst_ref=h_mate.at[0, rows],
            send_sem=h_send.at[1], recv_sem=h_sem.at[1],
            device_id=cousin(step), device_id_type=MESH,
        )

    loads[0].wait()
    loads[1].wait()

    def make_g(begin, size):
        rows = pl.ds(begin, size)
        g_buf[rows] = (a_buf[rows].astype(F32) * b_buf[rows].astype(F32)).astype(BF16)

    def first_g(step):
        make_g((me ^ step) * own + HALF, own - HALF)
        move_g(0, step).start()
    @pl.loop(0, ROWS // 2)
    def _(at):
        step = (at // 2) * 4 + at % 2
        first_g(step + 2)

        @pl.when(at > 0)
        def _():
            first_g(step)
            move_u(0, step).start()
    for copy in loads[2:] + keep_u:
        copy.start()
    make_g(me * own + HALF, own - HALF)

    def send_part(part, also=None):
        @pl.loop(0, ROWS // 2)
        def _(at):
            step = (at // 2) * 4 + at % 2
            move_g(part, step + 2).start()
            if PARTS[part][0] == "all":
                move_u(part, step + 2).start()

            @pl.when(at > 0)
            def _():
                move_u(part, step).start()
                move_g(part, step).start()
                if also is not None:
                    move_y(also, step).start()

    give_h.wait_recv()
    for step in range(1, PIECES):
        share_h(step).start()
    send_part(1)

    @pl.loop(0, ROWS)
    def _(to):
        make_g(to * own, HALF)
    send_part(2)
    keep_g = [
        pltpu.make_async_copy(
            g_buf.at[kept(name, size, base_of(name, slot))],
            g_recv.at[me, pl.ds(slot, size)],
            local_sem.at[3 + COUNT + part],
        )
        for part, (name, slot, size) in enumerate(PARTS)
    ]
    for copy in keep_g:
        copy.start()

    @pl.loop(0, ROWS // 2)
    def _(at):
        u_recv[(at // 2) * 4 + 2 * (1 - side) + at % 2, HALF:] = jnp.zeros((SLOTS - HALF, LANES), BF16)

    for copy in loads[2:]:
        copy.wait()
    @pl.loop(0, own // 16)
    def _(at):
        rows = pl.ds(at * 16, 16)
        put = pl.ds(at * 16 + (at // (HALF // 16)) * HALF, 16)
        spec = split_rows([h_buf[rows, j * LANES : (j + 1) * LANES] for j in range(ROWS)])
        for k, (re, im) in enumerate(spec):
            h_first[k, put, :LANES] = re.astype(BF16)
            h_first[k, put, LANES:] = im.astype(BF16)

    def spectrum(begin, size):
        @pl.loop(0, ROWS)
        def _(k):
            rows = pl.ds(begin, size)
            h_spec[k, rows] = jnp.dot(
                h_first[k, rows], ahead_ref[k], preferred_element_type=F32
            ) * (1.0 / (ROWS * LANES))

    spectrum(0, HALF)
    spectrum(OWN, HALF)

    def mate_taps():
        all_of(h_mate.at[0, pl.ds(0, (PIECES - 1) * height)], h_sem.at[1])

        @pl.loop(0, HALF // 16)
        def _(at):
            rows = pl.ds(at * 16, 16)
            put = pl.ds(MATE + at * 16, 16)
            spec = split_rows(
                [h_mate[0, rows, j * LANES : (j + 1) * LANES].astype(F32) for j in range(ROWS)]
            )
            for k, (re, im) in enumerate(spec):
                h_first[k, put, :LANES] = re.astype(BF16)
                h_first[k, put, LANES:] = im.astype(BF16)
        spectrum(MATE, HALF)

    def compute(part):
        name, base, size = PARTS[part]

        @pl.loop(0, size // 16)
        def _(at):
            rows = pl.ds(base + at * 16, 16)
            for place, source in enumerate((g_recv, u_recv)):
                spec = split_rows([source[j, rows].astype(F32) for j in range(ROWS)])
                put = pl.ds(place * size + at * 16, 16)
                for k, (re, im) in enumerate(spec):
                    first[k, put, :LANES] = re.astype(BF16)
                    first[k, put, LANES:] = im.astype(BF16)

        @pl.loop(0, ROWS, unroll=2)
        def _(k):
            spec = jnp.dot(first[k, : 2 * size], ahead_ref[k], preferred_element_type=F32)
            gr, gi = spec[:size, :LANES], spec[:size, LANES:]
            ur, ui = spec[size:, :LANES], spec[size:, LANES:]
            hr = h_spec[k, pl.ds(base, size), :LANES]
            hi = h_spec[k, pl.ds(base, size), LANES:]
            to_input = jnp.concatenate([hr * gr + hi * gi, hr * gi - hi * gr], axis=1)
            to_filter = jnp.concatenate([gr * ur + gi * ui, gi * ur - gr * ui], axis=1)
            both = jnp.concatenate([to_input, to_filter], axis=0).astype(BF16)
            last[k, : 2 * size] = jnp.dot(both, back_ref[k], preferred_element_type=F32)

        @pl.loop(0, size // 16)
        def _(at):
            rows = pl.ds(base + at * 16, 16)
            for place in range(2):
                take = pl.ds(place * size + at * 16, 16)
                out = merge_rows([(last[k, take, :LANES], last[k, take, LANES:]) for k in range(ROWS)])
                for j in range(ROWS):
                    if place == 0:
                        y_buf[j, rows] = out[j].astype(BF16)
                    else:
                        f_buf[(j // 4) * 2 + j % 2, (j // 2) % 2, rows] = out[j].astype(BF16)

    def slots(part):
        return pl.ds(PARTS[part][1], PARTS[part][2])

    def sum_cousins(part, step):
        return pltpu.make_async_remote_copy(
            src_ref=f_buf.at[piece ^ step, :, slots(part)],
            dst_ref=f_recv.at[step, :, slots(part)],
            send_sem=s1.at[part], recv_sem=r1.at[part],
            device_id=cousin(step), device_id_type=MESH,
        )

    sum_mate = pltpu.make_async_remote_copy(
        src_ref=f_give, dst_ref=f_take, send_sem=s2, recv_sem=r2,
        device_id=across, device_id_type=MESH,
    )

    def sum_z(part):
        return pltpu.make_async_remote_copy(
            src_ref=f_send.at[slots(part)], dst_ref=f_last.at[slots(part)],
            send_sem=s3.at[part], recv_sem=r3.at[part],
            device_id=other_z, device_id_type=MESH,
        )

    def held(part, half):
        name, slot, size = PARTS[part]
        total = f_buf[piece, half, slots(part)].astype(F32)
        for step in range(1, PIECES):
            total = total + f_recv[step, half, slots(part)].astype(F32)
        if name == "own":
            total = total + f_take[half].astype(F32)
        return total

    def after_cousins(part):
        all_of(f_recv.at[pl.ds(1, PIECES - 1), :, slots(part)], r1.at[part])
        name = PARTS[part][0]
        if name == "mate":
            for half in range(2):
                f_give[half] = held(part, half).astype(BF16)
            sum_mate.start()
        else:
            if name == "own":
                sum_mate.wait()
            f_send[slots(part)] = held(part, 1 - z_hi).astype(BF16)
            sum_z(part).start()

    def after_z(part):
        name, slot, size = PARTS[part]
        sum_z(part).wait()
        f_ref[pl.ds(base_of(name, slot), size)] = (
            held(part, z_hi) + f_last[slots(part)].astype(F32)
        ) * scale

    def keep_y(part):
        name, slot, size = PARTS[part]
        return pltpu.make_async_copy(
            y_buf.at[me, pl.ds(slot, size)],
            y_ref.at[kept(name, size, base_of(name, slot))],
            local_sem.at[3 + 2 * COUNT + part],
        )

    def begin(part):
        all_of(blocks(part, True), g_sem.at[part])
        all_of(blocks(part), u_sem.at[part])
        keep_g[part].wait()
        keep_u[part].wait()
        if PARTS[part][0] == "mate":
            mate_taps()
        compute(part)
        for step in range(1, PIECES):
            sum_cousins(part, step).start()
        keep_y(part).start()

    begin(0)
    send_part(3, also=0)
    begin(1)
    begin(2)
    each_step(lambda step: move_y(2, step).start())
    near_step(lambda step: move_y(1, step).start())
    after_cousins(1)
    begin(3)
    after_cousins(2)
    after_cousins(0)
    each_step(lambda step: move_y(3, step).start())
    after_cousins(3)
    after_z(0)
    after_z(2)
    after_z(3)

    give_h.wait_send()
    all_of(h_mate.at[0, pl.ds(0, (PIECES - 1) * height)], h_send.at[1])
    for part in range(COUNT):
        keep_y(part).wait()
        all_of(f_recv.at[pl.ds(1, PIECES - 1), :, slots(part)], s1.at[part])
        all_of(blocks(part, True), g_send.at[part])
        all_of(blocks(part), u_send.at[part])
        all_of(blocks(part), y_send.at[part])
        all_of(blocks(part), y_sem.at[part])


def on_device(saved_input, out_gate, grad_out, long_filter):
    _, channels, width = saved_input.shape
    own, length = long_filter.shape
    scale = 1.0 / (math.sqrt(lax.axis_size("dp") * length) * ROWS * LANES)
    ahead, back = twiddled_tables()
    in_hbm = pl.BlockSpec(memory_space=pl.ANY)
    in_vmem = pl.BlockSpec(memory_space=pltpu.VMEM)
    dma = pltpu.SemaphoreType.DMA

    def run(*operands):
        return pl.pallas_call(
            lambda *refs: kernel(scale, *refs),
            out_shape=(
                pltpu.VMEM((channels, width), BF16),
                pltpu.VMEM((own, width), F32),
            ),
            in_specs=[in_hbm] * 6,
            out_specs=(in_vmem, in_vmem),
            scratch_shapes=[
                pltpu.VMEM(ahead.shape, BF16),
                pltpu.VMEM(back.shape, BF16),
                pltpu.VMEM((channels, width), BF16),
                pltpu.VMEM((channels, width), BF16),
                pltpu.VMEM((channels, width), BF16),
                pltpu.VMEM((own, length), F32),
                pltpu.VMEM((HALF // PIECES, length), F32),
                pltpu.VMEM((2, HALF, length), BF16),
                pltpu.VMEM((ROWS, SLOTS, width), BF16),
                pltpu.VMEM((ROWS, SLOTS, width), BF16),
                pltpu.VMEM((ROWS, SLOTS, 2 * LANES), BF16),
                pltpu.VMEM((ROWS, SLOTS, 2 * LANES), F32),
                pltpu.VMEM((ROWS, 2 * MOST, 2 * LANES), BF16),
                pltpu.VMEM((ROWS, 2 * MOST, 2 * LANES), F32),
                pltpu.VMEM((ROWS, SLOTS, width), BF16),
                pltpu.VMEM((PIECES, 2, SLOTS, LANES), BF16),
                pltpu.VMEM((PIECES, 2, SLOTS, LANES), BF16),
                pltpu.VMEM((2, HALF, LANES), BF16),
                pltpu.VMEM((2, HALF, LANES), BF16),
                pltpu.VMEM((SLOTS, LANES), BF16),
                pltpu.VMEM((SLOTS, LANES), BF16),
                dma((6 + 3 * COUNT,)),
                dma((2,)), dma((2,)),
                dma((COUNT,)), dma((COUNT,)),
                dma((COUNT,)), dma((COUNT,)),
                dma((COUNT,)), dma((COUNT,)),
                dma((COUNT,)), dma((COUNT,)),
                dma, dma,
                dma((COUNT,)), dma((COUNT,)),
            ],
            compiler_params=pltpu.CompilerParams(
                collective_id=0, has_side_effects=True, vmem_limit_bytes=58 * 2**20
            ),
        )(*operands)

    grad_input, grad_filter = run(
        saved_input[0], out_gate[0], grad_out[0], long_filter, jnp.asarray(ahead), jnp.asarray(back)
    )
    return grad_input[None], grad_filter


def solution(mesh):
    in_specs = (P("dp", None, "ctx"), P("dp", None, "ctx"), P("dp", None, "ctx"), P("ctx", None))
    out_specs = (P("dp", None, "ctx"), P("ctx", "dp"))
    return jax.shard_map(
        on_device, mesh=mesh, in_specs=in_specs, out_specs=out_specs, check_vma=False
    )
```

```python
import math

import jax
import jax.numpy as jnp
import numpy as np
from jax import lax
from jax.experimental import pallas as pl
from jax.experimental.pallas import tpu as pltpu
from jax.sharding import PartitionSpec as P

MESH = pl.DeviceIdType.MESH
LANES = 128
ROWS = 16
HALF = 128
MATE, OWN, SLOTS = HALF, 2 * HALF, 3 * HALF
PARTS = (("own", OWN, 128), ("mate", MATE, 128), ("all", 0, 64), ("all", 64, 64))
COUNT = len(PARTS)
MOST = max(size for _, _, size in PARTS)
PIECES = 8
F32 = jnp.float32
BF16 = jnp.bfloat16


def twiddled_tables():
    k = np.arange(ROWS)[:, None, None]
    n = np.arange(LANES)[None, :, None]
    m = np.arange(LANES)[None, None, :]
    points = 2 * ROWS * LANES
    turns = (n * (2 * (k + 2 * ROWS * m) + 1)) % (2 * points)
    angle = turns * (math.pi / points)
    cos, sin = np.cos(angle), np.sin(angle)
    ahead = np.concatenate(
        [np.concatenate([cos, -sin], axis=2), np.concatenate([sin, cos], axis=2)], axis=1
    )
    return ahead.astype(BF16), np.swapaxes(ahead, 1, 2).astype(BF16)


def split_rows(rows):
    count = len(rows)
    if count == 2:
        turned = rows[1] * math.cos(math.pi / 4)
        return [(rows[0] + turned, -turned), (rows[0] - turned, -turned)]
    even, odd = split_rows(rows[0::2]), split_rows(rows[1::2])
    out = [None] * count
    for k in range(count // 2):
        angle = math.pi * (2 * k + 1) / (2 * count)
        wr, wi = math.cos(angle), -math.sin(angle)
        (er, ei), (pr, pi) = even[k], odd[k]
        tr, ti = wr * pr - wi * pi, wr * pi + wi * pr
        out[k] = (er + tr, ei + ti)
        out[count - 1 - k] = (er - tr, ti - ei)
    return out


def merge_rows(spec):
    count = len(spec)
    if count == 2:
        (a, b), (c, d) = spec
        return [a + c, (a - c - b - d) * math.cos(math.pi / 4)]
    even, odd = [], []
    for k in range(count // 2):
        angle = math.pi * (2 * k + 1) / (2 * count)
        wr, wi = math.cos(angle), -math.sin(angle)
        (pr, pi), (qr, qi) = spec[k], spec[count - 1 - k]
        dr, di = pr - qr, pi + qi
        even.append((pr + qr, pi - qi))
        odd.append((wr * dr + wi * di, wr * di - wi * dr))
    out = [None] * count
    out[0::2], out[1::2] = merge_rows(even), merge_rows(odd)
    return out


def kernel(
    scale,
    u_ref, a_ref, b_ref, h_ref, ahead_hbm, back_hbm,
    y_ref, f_ref,
    ahead_ref, back_ref, a_buf, b_buf, g_buf, h_buf, h_piece, h_mate, u_recv, g_recv, h_first, h_spec, first, last, y_buf,
    f_buf, f_recv, f_give, f_take, f_send, f_last,
    local_sem, h_send, h_sem, u_send, u_sem, g_send, g_sem, y_send, y_sem,
    s1, r1, s2, r2, s3, r3,
):
    own = f_ref.shape[0]
    dp, me = lax.axis_index("dp"), lax.axis_index("ctx")
    core, z_hi, x = dp % 2, (dp // 2) % 2, dp // 4
    side = (me // 2) % 2
    piece = x * 2 + core

    def cousin(step):
        return ((x ^ (step // 2)) * 4 + z_hi * 2 + (core ^ (step % 2)), me)

    other_z = (dp + 2 - 4 * z_hi, me)
    across = (dp + 2 - 4 * z_hi, me ^ 2)

    def each_step(run):
        @pl.loop(1, ROWS)
        def _(step):
            run(step)

    def near_step(run):
        @pl.loop(1, ROWS // 2)
        def _(at):
            run((at // 2) * 4 + at % 2)

    barrier = pltpu.get_barrier_semaphore()

    def greet(peer):
        pl.semaphore_signal(barrier, inc=1, device_id=peer, device_id_type=MESH)

    each_step(lambda step: greet((dp, me ^ step)))
    for step in range(1, PIECES):
        greet(cousin(step))

    def kept(name, size, base):
        owner = me ^ 2 if name == "mate" else me
        return pl.ds(owner * own + base, size)

    def base_of(name, slot):
        return slot - OWN + HALF if name == "own" else slot

    height = HALF // PIECES
    load_piece = pltpu.make_async_copy(
        h_ref.at[pl.ds(HALF + piece * height, height)], h_piece, local_sem.at[3 + 3 * COUNT]
    )
    load_piece.start()
    loads = [
        pltpu.make_async_copy(a_ref, a_buf, local_sem.at[0]),
        pltpu.make_async_copy(b_ref, b_buf, local_sem.at[1]),
        pltpu.make_async_copy(h_ref, h_buf, local_sem.at[2]),
        pltpu.make_async_copy(ahead_hbm, ahead_ref, local_sem.at[4 + 3 * COUNT]),
        pltpu.make_async_copy(back_hbm, back_ref, local_sem.at[5 + 3 * COUNT]),
    ]
    keep_u = [
        pltpu.make_async_copy(
            u_ref.at[kept(name, size, base_of(name, slot))],
            u_recv.at[me, pl.ds(slot, size)],
            local_sem.at[3 + part],
        )
        for part, (name, slot, size) in enumerate(PARTS)
    ]
    for copy in loads[:2]:
        copy.start()

    for peer in (other_z, across):
        greet(peer)
    pl.semaphore_wait(barrier, ROWS - 1 + PIECES - 1 + 2)

    def exchange(src, dst, send, recv, part, step):
        name, slot, size = PARTS[part]
        owner = me ^ step ^ 2 if name == "mate" else me ^ step
        return pltpu.make_async_remote_copy(
            src_ref=src.at[pl.ds(owner * own + base_of(name, slot), size)],
            dst_ref=dst.at[me, pl.ds(slot, size)],
            send_sem=send.at[part],
            recv_sem=recv.at[part],
            device_id=(dp, me ^ step),
            device_id_type=MESH,
        )

    def move_u(part, step):
        return exchange(u_ref, u_recv, u_send, u_sem, part, step)

    def move_g(part, step):
        return exchange(g_buf, g_recv, g_send, g_sem, part, step)

    def move_y(part, step):
        name, slot, size = PARTS[part]
        return pltpu.make_async_remote_copy(
            src_ref=y_buf.at[me ^ step, pl.ds(slot, size)],
            dst_ref=y_ref.at[kept(name, size, base_of(name, slot))],
            send_sem=y_send.at[part],
            recv_sem=y_sem.at[part],
            device_id=(dp, me ^ step),
            device_id_type=MESH,
        )

    def all_of(ref, sem):
        pltpu.make_async_copy(ref, ref, sem).wait()

    def blocks(part, whole=False):
        name, slot, size = PARTS[part]
        count = ROWS - 1 if whole or name == "all" else ROWS // 2 - 1
        return g_recv.at[pl.ds(0, count), pl.ds(slot, size)]

    load_piece.wait()
    for j in range(ROWS):
        lanes = slice(j * LANES, (j + 1) * LANES)
        h_mate[1, :height, lanes] = h_piece[:, lanes].astype(BF16)

    give_h = pltpu.make_async_remote_copy(
        src_ref=h_mate.at[1, pl.ds(0, height)],
        dst_ref=h_mate.at[0, pl.ds(piece * height, height)],
        send_sem=h_send.at[0], recv_sem=h_sem.at[0],
        device_id=across, device_id_type=MESH,
    )
    give_h.start()

    def share_h(step):
        rows = pl.ds(piece * height, height)
        return pltpu.make_async_remote_copy(
            src_ref=h_mate.at[0, rows], dst_ref=h_mate.at[0, rows],
            send_sem=h_send.at[1], recv_sem=h_sem.at[1],
            device_id=cousin(step), device_id_type=MESH,
        )

    loads[0].wait()
    loads[1].wait()

    def make_g(begin, size):
        rows = pl.ds(begin, size)
        g_buf[rows] = (a_buf[rows].astype(F32) * b_buf[rows].astype(F32)).astype(BF16)

    def first_g(step):
        make_g((me ^ step) * own + HALF, own - HALF)
        move_g(0, step).start()
    @pl.loop(0, ROWS // 2)
    def _(at):
        step = (at // 2) * 4 + at % 2
        first_g(step + 2)

        @pl.when(at > 0)
        def _():
            first_g(step)
            move_u(0, step).start()
    for copy in loads[2:] + keep_u:
        copy.start()
    make_g(me * own + HALF, own - HALF)

    def send_part(part, also=None):
        @pl.loop(0, ROWS // 2)
        def _(at):
            step = (at // 2) * 4 + at % 2
            move_g(part, step + 2).start()
            if PARTS[part][0] == "all":
                move_u(part, step + 2).start()

            @pl.when(at > 0)
            def _():
                move_u(part, step).start()
                move_g(part, step).start()
                if also is not None:
                    move_y(also, step).start()

    give_h.wait_recv()
    for step in range(1, PIECES):
        share_h(step).start()
    send_part(1)

    @pl.loop(0, ROWS)
    def _(to):
        make_g(to * own, HALF)
    send_part(2)
    keep_g = [
        pltpu.make_async_copy(
            g_buf.at[kept(name, size, base_of(name, slot))],
            g_recv.at[me, pl.ds(slot, size)],
            local_sem.at[3 + COUNT + part],
        )
        for part, (name, slot, size) in enumerate(PARTS)
    ]
    for copy in keep_g:
        copy.start()

    @pl.loop(0, ROWS // 2)
    def _(at):
        u_recv[(at // 2) * 4 + 2 * (1 - side) + at % 2, HALF:] = jnp.zeros((SLOTS - HALF, LANES), BF16)

    for copy in loads[2:]:
        copy.wait()
    @pl.loop(0, own // 16)
    def _(at):
        rows = pl.ds(at * 16, 16)
        put = pl.ds(at * 16 + (at // (HALF // 16)) * HALF, 16)
        spec = split_rows([h_buf[rows, j * LANES : (j + 1) * LANES] for j in range(ROWS)])
        for k, (re, im) in enumerate(spec):
            h_first[k, put, :LANES] = re.astype(BF16)
            h_first[k, put, LANES:] = im.astype(BF16)

    def spectrum(begin, size):
        @pl.loop(0, ROWS)
        def _(k):
            rows = pl.ds(begin, size)
            h_spec[k, rows] = jnp.dot(
                h_first[k, rows], ahead_ref[k], preferred_element_type=F32
            ) * (1.0 / (ROWS * LANES))

    spectrum(0, HALF)
    spectrum(OWN, HALF)

    def mate_taps():
        all_of(h_mate.at[0, pl.ds(0, (PIECES - 1) * height)], h_sem.at[1])

        @pl.loop(0, HALF // 16)
        def _(at):
            rows = pl.ds(at * 16, 16)
            put = pl.ds(MATE + at * 16, 16)
            spec = split_rows(
                [h_mate[0, rows, j * LANES : (j + 1) * LANES].astype(F32) for j in range(ROWS)]
            )
            for k, (re, im) in enumerate(spec):
                h_first[k, put, :LANES] = re.astype(BF16)
                h_first[k, put, LANES:] = im.astype(BF16)
        spectrum(MATE, HALF)

    def compute(part):
        name, base, size = PARTS[part]

        @pl.loop(0, size // 16)
        def _(at):
            rows = pl.ds(base + at * 16, 16)
            for place, source in enumerate((g_recv, u_recv)):
                spec = split_rows([source[j, rows].astype(F32) for j in range(ROWS)])
                put = pl.ds(place * size + at * 16, 16)
                for k, (re, im) in enumerate(spec):
                    first[k, put, :LANES] = re.astype(BF16)
                    first[k, put, LANES:] = im.astype(BF16)

        @pl.loop(0, ROWS, unroll=2)
        def _(k):
            spec = jnp.dot(first[k, : 2 * size], ahead_ref[k], preferred_element_type=F32)
            gr, gi = spec[:size, :LANES], spec[:size, LANES:]
            ur, ui = spec[size:, :LANES], spec[size:, LANES:]
            hr = h_spec[k, pl.ds(base, size), :LANES]
            hi = h_spec[k, pl.ds(base, size), LANES:]
            to_input = jnp.concatenate([hr * gr + hi * gi, hr * gi - hi * gr], axis=1)
            to_filter = jnp.concatenate([gr * ur + gi * ui, gi * ur - gr * ui], axis=1)
            both = jnp.concatenate([to_input, to_filter], axis=0).astype(BF16)
            last[k, : 2 * size] = jnp.dot(both, back_ref[k], preferred_element_type=F32)

    def merge(part, place):
        name, base, size = PARTS[part]

        @pl.loop(0, size // 16)
        def _(at):
            rows = pl.ds(base + at * 16, 16)
            take = pl.ds(place * size + at * 16, 16)
            out = merge_rows([(last[k, take, :LANES], last[k, take, LANES:]) for k in range(ROWS)])
            for j in range(ROWS):
                if place == 0:
                    y_buf[j, rows] = out[j].astype(BF16)
                else:
                    f_buf[(j // 4) * 2 + j % 2, (j // 2) % 2, rows] = out[j].astype(BF16)

    def slots(part):
        return pl.ds(PARTS[part][1], PARTS[part][2])

    def sum_cousins(part, step):
        return pltpu.make_async_remote_copy(
            src_ref=f_buf.at[piece ^ step, :, slots(part)],
            dst_ref=f_recv.at[step, :, slots(part)],
            send_sem=s1.at[part], recv_sem=r1.at[part],
            device_id=cousin(step), device_id_type=MESH,
        )

    sum_mate = pltpu.make_async_remote_copy(
        src_ref=f_give, dst_ref=f_take, send_sem=s2, recv_sem=r2,
        device_id=across, device_id_type=MESH,
    )

    def sum_z(part):
        return pltpu.make_async_remote_copy(
            src_ref=f_send.at[slots(part)], dst_ref=f_last.at[slots(part)],
            send_sem=s3.at[part], recv_sem=r3.at[part],
            device_id=other_z, device_id_type=MESH,
        )

    def held(part, half):
        name, slot, size = PARTS[part]
        total = f_buf[piece, half, slots(part)].astype(F32)
        for step in range(1, PIECES):
            total = total + f_recv[step, half, slots(part)].astype(F32)
        if name == "own":
            total = total + f_take[half].astype(F32)
        return total

    def after_cousins(part):
        all_of(f_recv.at[pl.ds(1, PIECES - 1), :, slots(part)], r1.at[part])
        name = PARTS[part][0]
        if name == "mate":
            for half in range(2):
                f_give[half] = held(part, half).astype(BF16)
            sum_mate.start()
        else:
            if name == "own":
                sum_mate.wait()
            f_send[slots(part)] = held(part, 1 - z_hi).astype(BF16)
            sum_z(part).start()

    def after_z(part):
        name, slot, size = PARTS[part]
        sum_z(part).wait()
        f_ref[pl.ds(base_of(name, slot), size)] = (
            held(part, z_hi) + f_last[slots(part)].astype(F32)
        ) * scale

    def keep_y(part):
        name, slot, size = PARTS[part]
        return pltpu.make_async_copy(
            y_buf.at[me, pl.ds(slot, size)],
            y_ref.at[kept(name, size, base_of(name, slot))],
            local_sem.at[3 + 2 * COUNT + part],
        )

    def begin(part):
        all_of(blocks(part, True), g_sem.at[part])
        all_of(blocks(part), u_sem.at[part])
        keep_g[part].wait()
        keep_u[part].wait()
        if PARTS[part][0] == "mate":
            mate_taps()
        compute(part)
        merge(part, 1)
        for step in range(1, PIECES):
            sum_cousins(part, step).start()
        merge(part, 0)
        keep_y(part).start()

    begin(0)
    send_part(3, also=0)
    begin(1)
    begin(2)
    each_step(lambda step: move_y(2, step).start())
    near_step(lambda step: move_y(1, step).start())
    after_cousins(1)
    begin(3)
    after_cousins(2)
    after_cousins(0)
    each_step(lambda step: move_y(3, step).start())
    after_cousins(3)
    after_z(0)
    after_z(2)
    after_z(3)

    give_h.wait_send()
    all_of(h_mate.at[0, pl.ds(0, (PIECES - 1) * height)], h_send.at[1])
    for part in range(COUNT):
        keep_y(part).wait()
        all_of(f_recv.at[pl.ds(1, PIECES - 1), :, slots(part)], s1.at[part])
        all_of(blocks(part, True), g_send.at[part])
        all_of(blocks(part), u_send.at[part])
        all_of(blocks(part), y_send.at[part])
        all_of(blocks(part), y_sem.at[part])


def on_device(saved_input, out_gate, grad_out, long_filter):
    _, channels, width = saved_input.shape
    own, length = long_filter.shape
    scale = 1.0 / (math.sqrt(lax.axis_size("dp") * length) * ROWS * LANES)
    ahead, back = twiddled_tables()
    in_hbm = pl.BlockSpec(memory_space=pl.ANY)
    in_vmem = pl.BlockSpec(memory_space=pltpu.VMEM)
    dma = pltpu.SemaphoreType.DMA

    def run(*operands):
        return pl.pallas_call(
            lambda *refs: kernel(scale, *refs),
            out_shape=(
                pltpu.VMEM((channels, width), BF16),
                pltpu.VMEM((own, width), F32),
            ),
            in_specs=[in_hbm] * 6,
            out_specs=(in_vmem, in_vmem),
            scratch_shapes=[
                pltpu.VMEM(ahead.shape, BF16),
                pltpu.VMEM(back.shape, BF16),
                pltpu.VMEM((channels, width), BF16),
                pltpu.VMEM((channels, width), BF16),
                pltpu.VMEM((channels, width), BF16),
                pltpu.VMEM((own, length), F32),
                pltpu.VMEM((HALF // PIECES, length), F32),
                pltpu.VMEM((2, HALF, length), BF16),
                pltpu.VMEM((ROWS, SLOTS, width), BF16),
                pltpu.VMEM((ROWS, SLOTS, width), BF16),
                pltpu.VMEM((ROWS, SLOTS, 2 * LANES), BF16),
                pltpu.VMEM((ROWS, SLOTS, 2 * LANES), F32),
                pltpu.VMEM((ROWS, 2 * MOST, 2 * LANES), BF16),
                pltpu.VMEM((ROWS, 2 * MOST, 2 * LANES), F32),
                pltpu.VMEM((ROWS, SLOTS, width), BF16),
                pltpu.VMEM((PIECES, 2, SLOTS, LANES), BF16),
                pltpu.VMEM((PIECES, 2, SLOTS, LANES), BF16),
                pltpu.VMEM((2, HALF, LANES), BF16),
                pltpu.VMEM((2, HALF, LANES), BF16),
                pltpu.VMEM((SLOTS, LANES), BF16),
                pltpu.VMEM((SLOTS, LANES), BF16),
                dma((6 + 3 * COUNT,)),
                dma((2,)), dma((2,)),
                dma((COUNT,)), dma((COUNT,)),
                dma((COUNT,)), dma((COUNT,)),
                dma((COUNT,)), dma((COUNT,)),
                dma((COUNT,)), dma((COUNT,)),
                dma, dma,
                dma((COUNT,)), dma((COUNT,)),
            ],
            compiler_params=pltpu.CompilerParams(
                collective_id=0, has_side_effects=True, vmem_limit_bytes=58 * 2**20
            ),
        )(*operands)

    grad_input, grad_filter = run(
        saved_input[0], out_gate[0], grad_out[0], long_filter, jnp.asarray(ahead), jnp.asarray(back)
    )
    return grad_input[None], grad_filter


def solution(mesh):
    in_specs = (P("dp", None, "ctx"), P("dp", None, "ctx"), P("dp", None, "ctx"), P("ctx", None))
    out_specs = (P("dp", None, "ctx"), P("ctx", "dp"))
    return jax.shard_map(
        on_device, mesh=mesh, in_specs=in_specs, out_specs=out_specs, check_vma=False
    )
```
